32 devices in a mesh: seq: 8 (over z, x), head: 4 (over y, core).
Axes of the slice: x: 2, y: 2, z: 4, core: 2. Of those that a mesh axis runs over, the one named last changes fastest.
Arguments:
- inputs: bfloat16 [8192, 4096], P('seq', 'head'), as said below
- gate_input: bfloat16 [8192, 4096], P('seq', 'head'), may hold values from -6 to 6
- log_decay: float32 [8192, 64], P('seq', 'head'), as said below
- b_matrix: bfloat16 [8192, 4, 128], P('seq', 'head'), may hold values from -6 to 6
- c_matrix: bfloat16 [8192, 4, 128], P('seq', 'head'), may hold values from -1.25 to 1.25
- norm_gain: float32 [4096], P('head'), may hold values from 0.1 to 1.9
- cotangent: bfloat16 [8192, 4096], P('seq', 'head'), may hold values from -6 to 6
Outputs:
- normed: bfloat16 [8192, 4096], P('seq', 'head')
- grad_inputs: bfloat16 [8192, 4096], P('seq', 'head')
- grad_gate: bfloat16 [8192, 4096], P('seq', 'head')
- grad_decay: float32 [8192, 64], P('seq', 'head')
- grad_b_matrix: float32 [8192, 4, 128], P('seq', 'head')
- grad_c_matrix: float32 [8192, 4, 128], P('seq', 'head')
The draws below stay inside these ranges and needn't reach their ends.
Inputs may be any that keep to these rules, and one draw needn't show every extreme that they name: `log_decay`: every entry is strictly negative. `inputs`: real-valued and finite.
All inputs are finite; a program needn't handle non-finite values.
Results may differ from the reference program's by a relative error of at most 0.003.
Values sent between devices are 32-bit elements; how exact they have to be, the bound alone decides.
A program may use at most 192 MiB of HBM per device.

```python
import math
import jax
import jax.numpy as jnp
from jax import lax

TOK_DEV = 1024
SPAN = 128
P_SIZE = 64
N = 128
TOKEN_TOTAL = 8192
HEAD_TOTAL = 64
GROUPS = 4
WIDTH = 4096


def draw_inputs(key, part):
    key_values, key_cols = jax.random.split(key, 2)
    head_ids = (jnp.arange(WIDTH) // P_SIZE).astype(jnp.float32)
    ramp = head_ids / max(HEAD_TOTAL - 1, 1)
    column_scale = jnp.exp(jax.random.uniform(key_cols, (WIDTH,), minval=0.0, maxval=math.log(4.0)))
    values = jnp.clip(jax.random.normal(key_values, (TOKEN_TOTAL, WIDTH)), -5.0, 5.0)
    values = values * jnp.exp(ramp * math.log(3.0))[None, :]
    return (values * column_scale[None, :]).astype(jnp.bfloat16)


def draw_log_decay(key, part):
    random_subkeys = jax.random.split(key, 7)
    share_slow = 0.5
    slow_heads = jax.random.uniform(random_subkeys[0], (HEAD_TOTAL,)) < share_slow
    fast_rate = jnp.exp(jax.random.uniform(random_subkeys[1], (HEAD_TOTAL,), minval=math.log(1.0 / 50.0), maxval=math.log(1.0 / 30.0)))
    slow_rate = jnp.exp(jax.random.uniform(random_subkeys[2], (HEAD_TOTAL,), minval=math.log(0.1), maxval=math.log(0.5))) / TOKEN_TOTAL
    base_rate = jnp.where(slow_heads, slow_rate, fast_rate)
    shard_factor = jnp.exp(jax.random.uniform(random_subkeys[3], (TOKEN_TOTAL // TOK_DEV, HEAD_TOTAL), minval=math.log(0.5), maxval=math.log(2.0)))
    shard_factor = jnp.repeat(shard_factor, TOK_DEV, axis=0)
    token_factor = jax.random.uniform(random_subkeys[4], (TOKEN_TOTAL, HEAD_TOTAL), minval=0.5, maxval=1.5)
    decay_speed = -base_rate[None, :] * shard_factor * token_factor
    spike_row_list = jax.random.randint(random_subkeys[5], (3,), 0, TOKEN_TOTAL)
    spike_objective = jnp.log(jax.random.uniform(random_subkeys[6], (3, HEAD_TOTAL), minval=0.55, maxval=0.8))
    row_numbers = jnp.arange(TOKEN_TOTAL)[:, None]
    for spike_index in range(3):
        decay_speed = decay_speed + jnp.where(row_numbers == spike_row_list[spike_index], spike_objective[spike_index][None, :], 0.0)
    return decay_speed.astype(jnp.float32)


def block_scale(rng, extent, cuts, smallest, top_value):
    gain, own = 1.0, jax.random.fold_in(rng, 6)
    for position, parts in cuts:
        draws = jnp.exp(jax.random.uniform(jax.random.fold_in(own, position), (parts,), jnp.float32, smallest / len(cuts), top_value / len(cuts)))
        gain = gain * jnp.repeat(draws, extent[position] // parts).reshape([-1 if axis == position else 1 for axis in range(len(extent))])
    return gain


def bell_draw(key, extent, scale, limit, cuts=(), held_as=jnp.bfloat16):
    entries = scale * jax.random.normal(key, extent, jnp.float32)
    if cuts:
        entries = entries * block_scale(key, extent, cuts, -0.22, 0.18)
    return jnp.clip(entries, -limit, limit).astype(held_as)


def setup_inputs(seed: int = 0) -> dict:
    key_list = jax.random.split(jax.random.key(seed), 8)
    return {
        "inputs": draw_inputs(jax.random.fold_in(key_list[7], 71), 0),
        "gate_input": bell_draw(key_list[1], (TOKEN_TOTAL, WIDTH), 1.0, 6.0, ((0, 8), (1, 4))),
        "log_decay": draw_log_decay(jax.random.fold_in(key_list[7], 71), 0),
        "b_matrix": bell_draw(key_list[3], (TOKEN_TOTAL, GROUPS, N), 1.0, 6.0, ((0, 8), (1, 4))),
        "c_matrix": bell_draw(key_list[4], (TOKEN_TOTAL, GROUPS, N), 0.09, 1.25, ((0, 8), (1, 4))),
        "norm_gain": jnp.clip(1.0 + 0.18 * jax.random.normal(key_list[5], (WIDTH,), jnp.float32), 0.1, 1.9),
        "cotangent": bell_draw(key_list[6], (TOKEN_TOTAL, WIDTH), 1.0, 6.0, ((0, 8), (1, 4))),
    }


HIGHEST = lax.Precision.HIGHEST
EPSILON = 1e-05

def pair_scores(c_half, b_half):
    return jnp.einsum('kign,kjgn->kgij', c_half, b_half, preferred_element_type=jnp.float32)

def score_grads(grad_scores, b_blocks, c_blocks):
    grad_c = jnp.einsum('kgij,kjgn->kign', grad_scores, b_blocks, precision=HIGHEST)
    grad_b = jnp.einsum('kgij,kign->kjgn', grad_scores, c_blocks, precision=HIGHEST)
    return (grad_b, grad_c)

def span_core(x_blocks, a_blocks, b_blocks, c_blocks, scores):
    running = jnp.cumsum(jnp.moveaxis(a_blocks, 1, 3), axis=3)
    length = running.shape[3]
    row_numbers = lax.broadcasted_iota(jnp.int32, (length, length), 0)
    col_ids = lax.broadcasted_iota(jnp.int32, (length, length), 1)
    causal = row_numbers >= col_ids
    log_gaps = running[..., :, None] - running[..., None, :]
    decays = jnp.exp(jnp.where(causal, log_gaps, -1e+30))
    weighted = decays * scores[:, :, None]
    diagonal = jnp.einsum('kgrij,kjgrp->kigrp', weighted, x_blocks, precision=HIGHEST)
    span_end = running[..., -1]
    to_end = jnp.exp(span_end[..., None] - running)
    scaled = x_blocks * jnp.moveaxis(to_end, 3, 1)[..., None]
    block_states = jnp.einsum('kjgrp,kjgn->kgrpn', scaled, b_blocks, precision=HIGHEST)

    def advance(carried, paired):
        factor, fresh = paired
        return (factor[..., None, None] * carried + fresh, carried)
    empty_state = jnp.zeros(block_states.shape[1:], jnp.float32)
    final, starts = lax.scan(advance, empty_state, (jnp.exp(span_end), block_states))
    from_state = jnp.einsum('kign,kgrpn->kigrp', c_blocks, starts, precision=HIGHEST)
    ssd_out = diagonal + from_state * jnp.moveaxis(jnp.exp(running), 3, 1)[..., None]
    return (ssd_out, final, running, span_end)

def group_forward(x_blocks, a_blocks, b_blocks, c_blocks, scores):
    return span_core(x_blocks, a_blocks, b_blocks, c_blocks, scores)[0]

def group_apply(packed):
    x_blocks, a_blocks, b_blocks, c_blocks, b_half, c_half = packed
    return group_forward(x_blocks, a_blocks, b_blocks, c_blocks, pair_scores(c_half, b_half))

def group_backward(packed):
    x_blocks, a_blocks, b_blocks, c_blocks, b_half, c_half, upstream = packed
    scores = pair_scores(c_half, b_half)
    unused, pullback = jax.vjp(group_forward, x_blocks, a_blocks, b_blocks, c_blocks, scores)
    grad_x, grad_a, grad_b, grad_c, grad_scores = pullback(upstream)
    extra_b, extra_c = score_grads(grad_scores, b_blocks, c_blocks)
    return (grad_x, grad_a, grad_b + extra_b, grad_c + extra_c)

def reference(inputs, gate_input, log_decay, b_matrix, c_matrix, norm_gain, cotangent):
    tok_rows, width = inputs.shape
    head_count = log_decay.shape[1]
    groups = b_matrix.shape[1]
    state_size = b_matrix.shape[2]
    head_size = width // head_count
    per_group = head_count // groups
    blocks = tok_rows // SPAN
    x_groups = jnp.moveaxis(inputs.astype(jnp.float32).reshape(blocks, SPAN, groups, 1, per_group, head_size), 2, 0)
    a_groups = jnp.moveaxis(log_decay.reshape(blocks, SPAN, groups, 1, per_group), 2, 0)
    b_halves = jnp.moveaxis(b_matrix.reshape(blocks, SPAN, groups, 1, state_size), 2, 0)
    c_halves = jnp.moveaxis(c_matrix.reshape(blocks, SPAN, groups, 1, state_size), 2, 0)
    b_groups = b_halves.astype(jnp.float32)
    c_groups = c_halves.astype(jnp.float32)
    ssd_groups = lax.map(group_apply, (x_groups, a_groups, b_groups, c_groups, b_halves, c_halves))
    ssd_out = jnp.moveaxis(ssd_groups, 0, 2).reshape(tok_rows, width)
    gate_value = gate_input.astype(jnp.float32)
    sigmoid_gate = jax.nn.sigmoid(gate_value)
    gate_silu = gate_value * sigmoid_gate
    gated = ssd_out * gate_silu
    scaled_cot = norm_gain[None, :] * cotangent.astype(jnp.float32)
    squares = lax.optimization_barrier(jnp.sum(gated * gated, axis=1))
    products = lax.optimization_barrier(jnp.sum(gated * scaled_cot, axis=1))
    inverse_rms = lax.rsqrt(squares / width + EPSILON)
    normed = (gated * inverse_rms[:, None] * norm_gain[None, :]).astype(jnp.bfloat16)
    grad_gated = inverse_rms[:, None] * scaled_cot - gated * (inverse_rms ** 3 * products / width)[:, None]
    grad_gate = (grad_gated * ssd_out * sigmoid_gate * (1.0 + gate_value * (1.0 - sigmoid_gate))).astype(jnp.bfloat16)
    grad_ssd = grad_gated * gate_silu
    up_groups = jnp.moveaxis(grad_ssd.reshape(blocks, SPAN, groups, 1, per_group, head_size), 2, 0)
    grad_x, grad_a, grad_b, grad_c = lax.map(group_backward, (x_groups, a_groups, b_groups, c_groups, b_halves, c_halves, up_groups))
    grad_inputs = jnp.moveaxis(grad_x, 0, 2).reshape(tok_rows, width).astype(jnp.bfloat16)
    grad_decay = jnp.moveaxis(grad_a, 0, 2).reshape(tok_rows, head_count)
    grad_b_matrix = jnp.moveaxis(grad_b, 0, 2).reshape(tok_rows, groups, state_size)
    grad_c_matrix = jnp.moveaxis(grad_c, 0, 2).reshape(tok_rows, groups, state_size)
    return (normed, grad_inputs, grad_gate, grad_decay, grad_b_matrix, grad_c_matrix)
```

```python
import functools

import jax
import jax.numpy as jnp
from jax import lax
from jax.experimental import pallas as pl
from jax.experimental.pallas import tpu as pltpu
from jax.sharding import PartitionSpec as P

SPAN = 128
EPSILON = 1e-05
F32 = jnp.float32
BF16 = jnp.bfloat16
VMEM_BYTES = 48 * 1024 * 1024


def split2(v):
    high = v.astype(BF16)
    return high, (v - high.astype(F32)).astype(BF16)


def split3(v):
    high, rest = v.astype(BF16), v
    rest = rest - high.astype(F32)
    mid = rest.astype(BF16)
    return high, mid, (rest - mid.astype(F32)).astype(BF16)


def dot(a, b, ca=1, cb=0):
    return lax.dot_general(a, b, (((ca,), (cb,)), ((), ())), preferred_element_type=F32)


def iotas(rows, cols):
    return (
        lax.broadcasted_iota(jnp.int32, (rows, cols), 0),
        lax.broadcasted_iota(jnp.int32, (rows, cols), 1),
    )


def spread_matrix(heads, width):
    row, col = iotas(heads, width)
    size = width // heads
    return jnp.where((col >= row * size) & (col < (row + 1) * size), 1.0, 0.0).astype(BF16)


def gather_matrix(heads, width):
    row, col = iotas(width, heads)
    size = width // heads
    return jnp.where((row >= col * size) & (row < (col + 1) * size), 1.0, 0.0).astype(BF16)


def spread(v, width):
    matrix = spread_matrix(v.shape[1], width)
    return sum(dot(p, matrix) for p in split3(v))


def head_sums(v, heads):
    matrix = gather_matrix(heads, v.shape[1])
    return sum(dot(p, matrix) for p in split3(v))


def running_sums(a):
    row, col = iotas(SPAN, SPAN)
    lower = jnp.where(row >= col, 1.0, 0.0).astype(BF16)
    return dot(jnp.concatenate([lower] * 3, 1), jnp.concatenate(split3(a), 0))


def state_terms(scaled, matrix_half):
    return dot(
        jnp.concatenate([matrix_half] * 2, 0), jnp.concatenate(split2(scaled), 0), 0, 0
    )


def read_state(matrix_half, state_parts):
    return dot(jnp.concatenate([matrix_half] * 2, 1), jnp.concatenate(state_parts, 0))


def local_state_kernel(x_ref, a_ref, b_ref, out_ref):
    width = x_ref.shape[1]
    size = b_ref.shape[1]

    @pl.when(pl.program_id(0) == 0)
    def _():
        out_ref[...] = jnp.zeros_like(out_ref)

    running = running_sums(a_ref[...])
    end = running[SPAN - 1 :, :]
    scaled = x_ref[...].astype(F32) * spread(jnp.exp(end - running), width)
    end_wide = spread(jnp.broadcast_to(end, (8, end.shape[1])), width)
    out_ref[:size, :] = out_ref[:size, :] * jnp.exp(end_wide[:1, :]) + state_terms(
        scaled, b_ref[...]
    )
    out_ref[size:, :] += end_wide


def pair_columns(pair_x, first):
    col = lax.broadcasted_iota(jnp.int32, pair_x.shape, 1)
    half = pair_x.shape[1] // 2
    keep = col < half if first else col >= half
    return jnp.where(keep, pair_x, jnp.zeros_like(pair_x))


def decays_of(running, running_rows, head, causal):
    gaps = running[:, head : head + 1] - running_rows[head : head + 1, :]
    return jnp.exp(jnp.where(causal, gaps, -1e30))


def rows_of(running):
    heads = running.shape[1]
    padded = jnp.concatenate([running, jnp.zeros((SPAN, SPAN - heads), F32)], 1)
    return jnp.transpose(padded)[:heads, :]


def diagonal_kernel(x_ref, a_ref, b_ref, c_ref, y_ref):
    heads = a_ref.shape[1]
    size = x_ref.shape[1] // heads
    running = running_sums(a_ref[...])
    running_rows = rows_of(running)
    row, col = iotas(SPAN, SPAN)
    causal = row >= col
    scores = dot(c_ref[...], b_ref[...], 1, 1)
    for pair in range(heads // 2):
        cols = slice(pair * 2 * size, (pair + 1) * 2 * size)
        x_pair = x_ref[:, cols]
        left, right = [], []
        for which in range(2):
            weighted = decays_of(running, running_rows, 2 * pair + which, causal) * scores
            left += list(split2(weighted))
            right += [pair_columns(x_pair, which == 0)] * 2
        y_ref[:, cols] = dot(jnp.concatenate(left, 1), jnp.concatenate(right, 0))


def carried(gathered_ref, size, reverse):
    count = gathered_ref.shape[0]
    place = lax.axis_index("seq")
    state = jnp.zeros((size, gathered_ref.shape[2]), F32)
    for hop in range(count - 1):
        source = count - 1 - hop if reverse else hop
        use = source > place if reverse else source < place
        later = jnp.exp(gathered_ref[source, size : size + 1, :]) * state
        state = jnp.where(use, later + gathered_ref[source, :size, :], state)
    return state


def silu_parts(gate_ref):
    gate = gate_ref[...].astype(F32)
    sigmoid = 1.0 / (1.0 + jnp.exp(-gate))
    return gate, sigmoid


def row_total(v):
    folded = v[:, :SPAN]
    for start in range(SPAN, v.shape[1], SPAN):
        folded = folded + v[:, start : start + SPAN]
    return jnp.sum(jnp.transpose(folded), axis=0, keepdims=True)


def forward_kernel(
    diag_ref, x_ref, a_ref, b_ref, c_ref, gate_ref, cot_ref, gain_ref, gathered_ref,
    y_ref, state_ref, sums_ref, carry,
):
    width = x_ref.shape[1]
    size = b_ref.shape[1]

    @pl.when(pl.program_id(0) == 0)
    def _():
        carry[...] = carried(gathered_ref, size, False)

    running = running_sums(a_ref[...])
    end = running[SPAN - 1 :, :]
    state = carry[...]
    state_ref[...] = state
    out = diag_ref[...] + spread(jnp.exp(running), width) * read_state(
        c_ref[...], split2(state)
    )
    y_ref[...] = out
    to_end = spread(jnp.exp(end - running), width)
    scaled = x_ref[...].astype(F32) * to_end
    end_wide = spread(jnp.broadcast_to(jnp.exp(end), (8, end.shape[1])), width)
    carry[...] = state * end_wide[:1, :] + state_terms(scaled, b_ref[...])
    gate, sigmoid = silu_parts(gate_ref)
    gated = out * (gate * sigmoid)
    scaled_cot = gain_ref[...] * cot_ref[...].astype(F32)
    squares = row_total(gated * gated)
    products = row_total(gated * scaled_cot)
    which = lax.broadcasted_iota(jnp.int32, sums_ref.shape, 0)
    sums_ref[...] = jnp.where(which == 0, squares, jnp.where(which == 1, products, 0.0))


def norm_kernel(
    full_width, y_ref, a_ref, c_ref, gate_ref, cot_ref, gain_ref, sums_ref,
    normed_ref, grad_gate_ref, up_ref, leaving_ref, before,
):
    width = y_ref.shape[1]

    @pl.when(pl.program_id(0) == 0)
    def _():
        leaving_ref[...] = jnp.zeros_like(leaving_ref)
        before[...] = jnp.zeros_like(before)

    sums = sums_ref[...]
    columns = jnp.transpose(
        jnp.concatenate([sums, jnp.zeros((SPAN - sums.shape[0], SPAN), F32)], 0)
    )
    squares, products = columns[:, 0:1], columns[:, 1:2]
    inverse_rms = lax.rsqrt(squares / full_width + EPSILON)
    factor = inverse_rms * inverse_rms * inverse_rms * products / full_width
    out = y_ref[...]
    gate, sigmoid = silu_parts(gate_ref)
    silu = gate * sigmoid
    gated = out * silu
    gain = gain_ref[...]
    normed_ref[...] = (gated * inverse_rms * gain).astype(BF16)
    grad_gated = inverse_rms * (gain * cot_ref[...].astype(F32)) - gated * factor
    grad_gate_ref[...] = (
        grad_gated * out * sigmoid * (1.0 + gate * (1.0 - sigmoid))
    ).astype(BF16)
    up = grad_gated * silu
    up_ref[...] = up
    running = running_sums(a_ref[...])
    reached = up * spread(jnp.exp(running), width)
    leaving_ref[...] += jnp.exp(before[:1, :]) * state_terms(reached, c_ref[...])
    end = running[SPAN - 1 :, :]
    before[...] += spread(jnp.broadcast_to(end, (8, end.shape[1])), width)


def diagonal_grad_kernel(
    x_ref, a_ref, b_ref, c_ref, up_ref, grad_x_ref, grad_b_ref, grad_c_ref
):
    heads = a_ref.shape[1]
    size = x_ref.shape[1] // heads
    running = running_sums(a_ref[...])
    running_rows = rows_of(running)
    row, col = iotas(SPAN, SPAN)
    causal = row >= col
    scores = dot(c_ref[...], b_ref[...], 1, 1)
    grad_scores = jnp.zeros((SPAN, SPAN), F32)
    for pair in range(heads // 2):
        cols = slice(pair * 2 * size, (pair + 1) * 2 * size)
        x_pair = x_ref[:, cols]
        high, low = split2(up_ref[:, cols])
        up_cat = jnp.concatenate([high, low], 1)
        left, right = [], []
        for which in range(2):
            decays = decays_of(running, running_rows, 2 * pair + which, causal)
            w_high, w_low = split2(decays * scores)
            x_half = pair_columns(x_pair, which == 0)
            grad_w = dot(up_cat, jnp.concatenate([x_half, x_half], 1), 1, 1)
            grad_scores = grad_scores + decays * grad_w
            u_high = pair_columns(high, which == 0)
            left += [w_high, w_low, w_high]
            right += [u_high, u_high, pair_columns(low, which == 0)]
        grad_x_ref[:, cols] = dot(
            jnp.concatenate(left, 0), jnp.concatenate(right, 0), 0, 0
        )
    g_high, g_low = split2(grad_scores)
    b_half, c_half = b_ref[...], c_ref[...]
    grad_c_ref[...] = dot(
        jnp.concatenate([g_high, g_low], 1), jnp.concatenate([b_half, b_half], 0)
    )
    grad_b_ref[...] = dot(
        jnp.concatenate([g_high, g_low], 0), jnp.concatenate([c_half, c_half], 0), 0, 0
    )


def wide_product(a_parts, b_parts):
    return (
        dot(a_parts[0], b_parts[0], 1, 1)
        + dot(a_parts[1], b_parts[0], 1, 1)
        + dot(a_parts[0], b_parts[1], 1, 1)
    )


def backward_kernel(
    x_ref, a_ref, b_ref, c_ref, up_ref, y_ref, state_ref, diag_ref, gathered_ref,
    leaving_ref, part_b_ref, part_c_ref,
    grad_x_ref, grad_a_ref, grad_b_ref, grad_c_ref, carry,
):
    heads = a_ref.shape[1]
    width = x_ref.shape[1]
    size = b_ref.shape[1]

    @pl.when(pl.program_id(0) == 0)
    def _():
        count = gathered_ref.shape[0]
        place = lax.axis_index("seq")
        adjoint = jnp.zeros((size, width), F32)
        for source in range(count - 1, 0, -1):
            later = jnp.exp(gathered_ref[source, :1, :]) * adjoint
            adjoint = jnp.where(source > place, later + leaving_ref[source], adjoint)
        carry[...] = adjoint

    x = x_ref[...].astype(F32)
    up = up_ref[...]
    b_half, c_half = b_ref[...], c_ref[...]
    running = running_sums(a_ref[...])
    end = running[SPAN - 1 :, :]
    reach = spread(jnp.exp(running), width)
    to_end = spread(jnp.exp(end - running), width)
    end_wide = reach[SPAN - 1 :, :]
    adjoint, state = carry[...], state_ref[...]
    adjoint_parts, state_parts = split2(adjoint), split2(state)
    scaled = x * to_end
    reached = up * reach
    scaled_parts, reached_parts = split2(scaled), split2(reached)
    grad_x = diag_ref[...] + to_end * read_state(b_half, adjoint_parts)
    grad_x_ref[...] = grad_x.astype(BF16)
    grad_c_ref[...] = part_c_ref[...] + wide_product(reached_parts, state_parts)
    grad_b_ref[...] = part_b_ref[...] + wide_product(scaled_parts, adjoint_parts)
    b_twice = jnp.concatenate([b_half, b_half], 0)
    state_end = end_wide * state + dot(b_twice, jnp.concatenate(scaled_parts, 0), 0, 0)
    last = jnp.sum(adjoint * state_end, axis=0, keepdims=True)
    c_twice = jnp.concatenate([c_half, c_half], 0)
    carry[...] = end_wide * adjoint + dot(
        c_twice, jnp.concatenate(reached_parts, 0), 0, 0
    )
    row = lax.broadcasted_iota(jnp.int32, (SPAN, width), 0)
    change = up * y_ref[...] - x * grad_x
    change = change + jnp.where(row == SPAN - 1, last, 0.0)
    grad_running = head_sums(change, heads)
    row, col = iotas(SPAN, SPAN)
    upper = jnp.where(row <= col, 1.0, 0.0).astype(BF16)
    grad_a_ref[...] = dot(
        jnp.concatenate([upper] * 3, 1), jnp.concatenate(split3(grad_running), 0)
    )


def per_device(inputs, gate_input, log_decay, b_matrix, c_matrix, norm_gain, cotangent):
    tokens, width = inputs.shape
    heads = log_decay.shape[1]
    size = b_matrix.shape[2]
    blocks = tokens // SPAN
    seq = lax.axis_size("seq")
    full_width = width * lax.axis_size("head")
    b_half = b_matrix.reshape(tokens, size)
    c_half = c_matrix.reshape(tokens, size)
    gain = norm_gain.reshape(1, width)

    def rows(cols, height=SPAN):
        return pl.BlockSpec((height, cols), lambda k: (k, 0))

    def back(cols):
        return pl.BlockSpec((SPAN, cols), lambda k: (blocks - 1 - k, 0))

    def whole(*shape):
        return pl.BlockSpec(shape, lambda k: (0,) * len(shape))

    def shape(*dims, dtype=F32):
        return jax.ShapeDtypeStruct(dims, dtype)

    def call(kernel, in_specs, out_specs, out_shape, flops, moved, scratch=()):
        return pl.pallas_call(
            kernel,
            grid=(blocks,),
            in_specs=in_specs,
            out_specs=out_specs,
            out_shape=out_shape,
            scratch_shapes=list(scratch),
            compiler_params=pltpu.CompilerParams(
                dimension_semantics=("arbitrary",), vmem_limit_bytes=VMEM_BYTES
            ),
            cost_estimate=pl.CostEstimate(
                flops=flops, bytes_accessed=moved, transcendentals=0
            ),
        )

    mega = 1 << 20
    carry = pltpu.VMEM((size, width), F32)
    local = call(
        local_state_kernel,
        [rows(width), rows(heads), rows(size)],
        whole(size + 8, width),
        shape(size + 8, width),
        600 * mega,
        3 * mega,
    )(inputs, log_decay, b_half)
    gathered = lax.all_gather(local, "seq")
    diagonal = call(
        diagonal_kernel,
        [rows(width), rows(heads), rows(size), rows(size)],
        rows(width),
        shape(tokens, width),
        5000 * mega,
        8 * mega,
    )(inputs, log_decay, b_half, c_half)
    ssd_out, states, sums = call(
        forward_kernel,
        [
            rows(width), rows(width), rows(heads), rows(size), rows(size), rows(width),
            rows(width), whole(1, width), whole(seq, size + 8, width),
        ],
        [rows(width), rows(width, size), rows(SPAN, 8)],
        [shape(tokens, width), shape(blocks * size, width), shape(blocks * 8, SPAN)],
        1500 * mega,
        20 * mega,
        [carry],
    )(diagonal, inputs, log_decay, b_half, c_half, gate_input, cotangent, gain, gathered)
    sums = lax.psum(sums, "head")
    normed, grad_gate, upstream, leaving = call(
        functools.partial(norm_kernel, full_width),
        [
            rows(width), rows(heads), rows(size), rows(width), rows(width),
            whole(1, width), rows(SPAN, 8),
        ],
        [rows(width), rows(width), rows(width), whole(size, width)],
        [
            shape(tokens, width, dtype=BF16), shape(tokens, width, dtype=BF16),
            shape(tokens, width), shape(size, width),
        ],
        1000 * mega,
        20 * mega,
        [pltpu.VMEM((8, width), F32)],
    )(ssd_out, log_decay, c_half, gate_input, cotangent, gain, sums)
    all_leaving = lax.all_gather(leaving, "seq")
    diagonal_grad, part_b, part_c = call(
        diagonal_grad_kernel,
        [rows(width), rows(heads), rows(size), rows(size), rows(width)],
        [rows(width), rows(size), rows(size)],
        [shape(tokens, width), shape(tokens, size), shape(tokens, size)],
        8000 * mega,
        12 * mega,
    )(inputs, log_decay, b_half, c_half, upstream)
    grad_x, grad_a, grad_b, grad_c = call(
        backward_kernel,
        [
            back(width), back(heads), back(size), back(size), back(width), back(width),
            pl.BlockSpec((size, width), lambda k: (blocks - 1 - k, 0)), back(width),
            pl.BlockSpec((seq, 8, width), lambda k: (0, size // 8, 0)),
            whole(seq, size, width), back(size), back(size),
        ],
        [back(width), back(heads), back(size), back(size)],
        [
            shape(tokens, width, dtype=BF16), shape(tokens, heads),
            shape(tokens, size), shape(tokens, size),
        ],
        3000 * mega,
        30 * mega,
        [carry],
    )(
        inputs, log_decay, b_half, c_half, upstream, ssd_out, states, diagonal_grad,
        gathered, all_leaving, part_b, part_c,
    )
    return (
        normed, grad_x, grad_gate, grad_a,
        grad_b.reshape(b_matrix.shape), grad_c.reshape(c_matrix.shape),
    )


def solution(mesh):
    wide = P("seq", "head")
    grouped = P("seq", "head", None)
    return jax.shard_map(
        per_device,
        mesh=mesh,
        in_specs=(wide, wide, wide, grouped, grouped, P("head"), wide),
        out_specs=(wide, wide, wide, wide, grouped, grouped),
        check_vma=False,
    )
```

```python
import functools

import jax
import jax.numpy as jnp
from jax import lax
from jax.experimental import pallas as pl
from jax.experimental.pallas import tpu as pltpu
from jax.sharding import PartitionSpec as P

SPAN = 128
EPSILON = 1e-05
F32 = jnp.float32
BF16 = jnp.bfloat16
VMEM_BYTES = 60 * 1024 * 1024


def split2(v):
    high = v.astype(BF16)
    return high, (v - high.astype(F32)).astype(BF16)


def split3(v):
    high, rest = v.astype(BF16), v
    rest = rest - high.astype(F32)
    mid = rest.astype(BF16)
    return high, mid, (rest - mid.astype(F32)).astype(BF16)


def dot(a, b, ca=1, cb=0):
    return lax.dot_general(a, b, (((ca,), (cb,)), ((), ())), preferred_element_type=F32)


def iotas(rows, cols):
    return (
        lax.broadcasted_iota(jnp.int32, (rows, cols), 0),
        lax.broadcasted_iota(jnp.int32, (rows, cols), 1),
    )


def spread_matrix(heads, width):
    row, col = iotas(heads, width)
    size = width // heads
    return jnp.where((col >= row * size) & (col < (row + 1) * size), 1.0, 0.0).astype(BF16)


def gather_matrix(heads, width):
    row, col = iotas(width, heads)
    size = width // heads
    return jnp.where((row >= col * size) & (row < (col + 1) * size), 1.0, 0.0).astype(BF16)


def spread(v, width, parts=split2):
    matrix = spread_matrix(v.shape[1], width)
    return sum(dot(p, matrix) for p in parts(v))


def head_sums(v, heads):
    matrix = gather_matrix(heads, v.shape[1])
    return sum(dot(p, matrix) for p in split2(v))


def running_sums(a):
    row, col = iotas(SPAN, SPAN)
    lower = jnp.where(row >= col, 1.0, 0.0).astype(BF16)
    return dot(jnp.concatenate([lower] * 3, 1), jnp.concatenate(split3(a), 0))


def state_terms(scaled, matrix_half):
    return dot(
        jnp.concatenate([matrix_half] * 2, 0), jnp.concatenate(split2(scaled), 0), 0, 0
    )


def read_state(matrix_half, state_parts):
    return dot(jnp.concatenate([matrix_half] * 2, 1), jnp.concatenate(state_parts, 0))


def local_state_kernel(x_ref, a_ref, b_ref, out_ref, total_ref):
    width = x_ref.shape[1]

    @pl.when(pl.program_id(0) == 0)
    def _():
        out_ref[...] = jnp.zeros_like(out_ref)
        total_ref[...] = jnp.zeros_like(total_ref)

    running = running_sums(a_ref[...])
    end = running[SPAN - 1 :, :]
    scaled = x_ref[...].astype(F32) * spread(jnp.exp(end - running), width)
    end_wide = spread(jnp.broadcast_to(end, (8, end.shape[1])), width, split3)
    out_ref[...] = out_ref[...] * jnp.exp(end_wide[:1, :]) + state_terms(
        scaled, b_ref[...]
    )
    total_ref[...] += end_wide


def pair_columns(pair_x, first):
    col = lax.broadcasted_iota(jnp.int32, pair_x.shape, 1)
    half = pair_x.shape[1] // 2
    keep = col < half if first else col >= half
    return jnp.where(keep, pair_x, jnp.zeros_like(pair_x))


def decays_of(running, running_rows, head, causal):
    gaps = running[:, head : head + 1] - running_rows[head : head + 1, :]
    return jnp.exp(jnp.where(causal, gaps, -1e30))


def rows_of(running):
    heads = running.shape[1]
    padded = jnp.concatenate([running, jnp.zeros((SPAN, SPAN - heads), F32)], 1)
    return jnp.transpose(padded)[:heads, :]


def diagonal_kernel(x_ref, a_ref, b_ref, c_ref, y_ref):
    heads = a_ref.shape[1]
    size = x_ref.shape[1] // heads
    running = running_sums(a_ref[...])
    running_rows = rows_of(running)
    row, col = iotas(SPAN, SPAN)
    causal = row >= col
    scores = dot(c_ref[...], b_ref[...], 1, 1)
    for pair in range(heads // 2):
        cols = slice(pair * 2 * size, (pair + 1) * 2 * size)
        x_pair = x_ref[:, cols]
        left, right = [], []
        for which in range(2):
            weighted = decays_of(running, running_rows, 2 * pair + which, causal) * scores
            left += list(split2(weighted))
            right += [pair_columns(x_pair, which == 0)] * 2
        y_ref[:, cols] = dot(jnp.concatenate(left, 1), jnp.concatenate(right, 0))


def chain_kernel(
    reverse, own_ref, total_ref, out_ref, landed, onward, send_sem, recv_sem
):
    count = lax.axis_size("seq")
    place = lax.axis_index("seq")
    up, down = lax.rem(place + 1, count), lax.rem(place + count - 1, count)
    first, last = place == 0, place == count - 1
    target, source = (down, up) if reverse else (up, down)
    starts, ends = (last, first) if reverse else (first, last)
    column = lax.axis_index("head")
    barrier = pltpu.get_barrier_semaphore()
    pl.semaphore_signal(
        barrier, inc=1, device_id=(source, column), device_id_type=pl.DeviceIdType.MESH
    )
    pl.semaphore_wait(barrier, 1)
    chunks = out_ref.shape[0] // 8

    def chunk(i):
        return pl.ds(pl.multiple_of(i * 8, 8), 8)

    def copy(i):
        return pltpu.make_async_remote_copy(
            src_ref=onward.at[chunk(i)],
            dst_ref=landed.at[chunk(i)],
            send_sem=send_sem.at[i],
            recv_sem=recv_sem.at[i],
            device_id=(target, column),
            device_id_type=pl.DeviceIdType.MESH,
        )

    @pl.when(starts)
    def _():
        out_ref[...] = jnp.zeros_like(out_ref)

    def step(i, nothing):
        @pl.when(jnp.logical_not(starts))
        def _():
            copy(i).wait_recv()
            out_ref[chunk(i), :] = landed[chunk(i), :]

        @pl.when(jnp.logical_not(ends))
        def _():
            decay = jnp.exp(total_ref[0:1, :])
            onward[chunk(i), :] = decay * out_ref[chunk(i), :] + own_ref[chunk(i), :]
            copy(i).start()

        return nothing

    lax.fori_loop(0, chunks, step, 0)

    @pl.when(jnp.logical_not(ends))
    def _():
        def finish(i, nothing):
            copy(i).wait_send()
            return nothing

        lax.fori_loop(0, chunks, finish, 0)


def chain(own, totals, reverse):
    rows, width = own.shape
    return pl.pallas_call(
        functools.partial(chain_kernel, reverse),
        out_shape=jax.ShapeDtypeStruct((rows, width), F32),
        in_specs=[pl.BlockSpec(memory_space=pltpu.VMEM)] * 2,
        out_specs=pl.BlockSpec(memory_space=pltpu.VMEM),
        scratch_shapes=[
            pltpu.VMEM((rows, width), F32),
            pltpu.VMEM((rows, width), F32),
            pltpu.SemaphoreType.DMA((rows // 8,)),
            pltpu.SemaphoreType.DMA((rows // 8,)),
        ],
        compiler_params=pltpu.CompilerParams(
            collective_id=1 if reverse else 0,
            has_side_effects=True,
            vmem_limit_bytes=VMEM_BYTES,
        ),
        cost_estimate=pl.CostEstimate(
            flops=1 << 20, bytes_accessed=4 << 20, transcendentals=0
        ),
    )(own, totals)


def silu_parts(gate_ref):
    gate = gate_ref[...].astype(F32)
    sigmoid = 1.0 / (1.0 + jnp.exp(-gate))
    return gate, sigmoid


def row_total(v):
    folded = v[:, :SPAN]
    for start in range(SPAN, v.shape[1], SPAN):
        folded = folded + v[:, start : start + SPAN]
    return jnp.sum(jnp.transpose(folded), axis=0, keepdims=True)


def forward_kernel(
    diag_ref, x_ref, a_ref, b_ref, c_ref, gate_ref, cot_ref, gain_ref, incoming_ref,
    y_ref, state_ref, sums_ref, carry,
):
    width = x_ref.shape[1]

    @pl.when(pl.program_id(0) == 0)
    def _():
        carry[...] = incoming_ref[...]

    running = running_sums(a_ref[...])
    end = running[SPAN - 1 :, :]
    state = carry[...]
    state_ref[...] = state
    out = diag_ref[...] + spread(jnp.exp(running), width) * read_state(
        c_ref[...], split2(state)
    )
    y_ref[...] = out
    to_end = spread(jnp.exp(end - running), width)
    scaled = x_ref[...].astype(F32) * to_end
    end_wide = spread(jnp.broadcast_to(jnp.exp(end), (8, end.shape[1])), width)
    carry[...] = state * end_wide[:1, :] + state_terms(scaled, b_ref[...])
    gate, sigmoid = silu_parts(gate_ref)
    gated = out * (gate * sigmoid)
    scaled_cot = gain_ref[...] * cot_ref[...].astype(F32)
    squares = row_total(gated * gated)
    products = row_total(gated * scaled_cot)
    which = lax.broadcasted_iota(jnp.int32, sums_ref.shape, 0)
    sums_ref[...] = jnp.where(which == 0, squares, jnp.where(which == 1, products, 0.0))


def norm_kernel(
    full_width, y_ref, a_ref, c_ref, gate_ref, cot_ref, gain_ref, sums_ref,
    normed_ref, grad_gate_ref, up_ref, leaving_ref, before,
):
    width = y_ref.shape[1]

    @pl.when(pl.program_id(0) == 0)
    def _():
        leaving_ref[...] = jnp.zeros_like(leaving_ref)
        before[...] = jnp.zeros_like(before)

    sums = sums_ref[...]
    columns = jnp.transpose(
        jnp.concatenate([sums, jnp.zeros((SPAN - sums.shape[0], SPAN), F32)], 0)
    )
    squares, products = columns[:, 0:1], columns[:, 1:2]
    inverse_rms = lax.rsqrt(squares / full_width + EPSILON)
    factor = inverse_rms * inverse_rms * inverse_rms * products / full_width
    out = y_ref[...]
    gate, sigmoid = silu_parts(gate_ref)
    silu = gate * sigmoid
    gated = out * silu
    gain = gain_ref[...]
    normed_ref[...] = (gated * inverse_rms * gain).astype(BF16)
    grad_gated = inverse_rms * (gain * cot_ref[...].astype(F32)) - gated * factor
    grad_gate_ref[...] = (
        grad_gated * out * sigmoid * (1.0 + gate * (1.0 - sigmoid))
    ).astype(BF16)
    up = grad_gated * silu
    up_ref[...] = up
    running = running_sums(a_ref[...])
    reached = up * spread(jnp.exp(running), width)
    leaving_ref[...] += jnp.exp(before[:1, :]) * state_terms(reached, c_ref[...])
    end = running[SPAN - 1 :, :]
    before[...] += spread(jnp.broadcast_to(end, (8, end.shape[1])), width, split3)


def diagonal_grad_kernel(
    x_ref, a_ref, b_ref, c_ref, up_ref, grad_x_ref, grad_b_ref, grad_c_ref
):
    heads = a_ref.shape[1]
    size = x_ref.shape[1] // heads
    running = running_sums(a_ref[...])
    running_rows = rows_of(running)
    row, col = iotas(SPAN, SPAN)
    causal = row >= col
    scores = dot(c_ref[...], b_ref[...], 1, 1)
    grad_scores = jnp.zeros((SPAN, SPAN), F32)
    for pair in range(heads // 2):
        cols = slice(pair * 2 * size, (pair + 1) * 2 * size)
        x_pair = x_ref[:, cols]
        high, low = split2(up_ref[:, cols])
        up_cat = jnp.concatenate([high, low], 1)
        left, right = [], []
        for which in range(2):
            decays = decays_of(running, running_rows, 2 * pair + which, causal)
            w_high, w_low = split2(decays * scores)
            x_half = pair_columns(x_pair, which == 0)
            grad_w = dot(up_cat, jnp.concatenate([x_half, x_half], 1), 1, 1)
            grad_scores = grad_scores + decays * grad_w
            u_high = pair_columns(high, which == 0)
            left += [w_high, w_low, w_high]
            right += [u_high, u_high, pair_columns(low, which == 0)]
        grad_x_ref[:, cols] = dot(
            jnp.concatenate(left, 0), jnp.concatenate(right, 0), 0, 0
        )
    g_high, g_low = split2(grad_scores)
    b_half, c_half = b_ref[...], c_ref[...]
    grad_c_ref[...] = dot(
        jnp.concatenate([g_high, g_low], 1), jnp.concatenate([b_half, b_half], 0)
    )
    grad_b_ref[...] = dot(
        jnp.concatenate([g_high, g_low], 0), jnp.concatenate([c_half, c_half], 0), 0, 0
    )


def wide_product(a_parts, b_parts):
    return (
        dot(a_parts[0], b_parts[0], 1, 1)
        + dot(a_parts[1], b_parts[0], 1, 1)
        + dot(a_parts[0], b_parts[1], 1, 1)
    )


def backward_kernel(
    x_ref, a_ref, b_ref, c_ref, up_ref, y_ref, state_ref, diag_ref, incoming_ref,
    part_b_ref, part_c_ref,
    grad_x_ref, grad_a_ref, grad_b_ref, grad_c_ref, carry,
):
    heads = a_ref.shape[1]
    width = x_ref.shape[1]

    @pl.when(pl.program_id(0) == 0)
    def _():
        carry[...] = incoming_ref[...]

    x = x_ref[...].astype(F32)
    up = up_ref[...]
    b_half, c_half = b_ref[...], c_ref[...]
    running = running_sums(a_ref[...])
    end = running[SPAN - 1 :, :]
    reach = spread(jnp.exp(running), width)
    to_end = spread(jnp.exp(end - running), width)
    end_wide = reach[SPAN - 1 :, :]
    adjoint, state = carry[...], state_ref[...]
    adjoint_parts, state_parts = split2(adjoint), split2(state)
    scaled = x * to_end
    reached = up * reach
    scaled_parts, reached_parts = split2(scaled), split2(reached)
    grad_x = diag_ref[...] + to_end * read_state(b_half, adjoint_parts)
    grad_x_ref[...] = grad_x.astype(BF16)
    grad_c_ref[...] = part_c_ref[...] + wide_product(reached_parts, state_parts)
    grad_b_ref[...] = part_b_ref[...] + wide_product(scaled_parts, adjoint_parts)
    b_twice = jnp.concatenate([b_half, b_half], 0)
    state_end = end_wide * state + dot(b_twice, jnp.concatenate(scaled_parts, 0), 0, 0)
    last = jnp.sum(adjoint * state_end, axis=0, keepdims=True)
    c_twice = jnp.concatenate([c_half, c_half], 0)
    carry[...] = end_wide * adjoint + dot(
        c_twice, jnp.concatenate(reached_parts, 0), 0, 0
    )
    row = lax.broadcasted_iota(jnp.int32, (SPAN, width), 0)
    change = up * y_ref[...] - x * grad_x
    change = change + jnp.where(row == SPAN - 1, last, 0.0)
    grad_running = head_sums(change, heads)
    row, col = iotas(SPAN, SPAN)
    upper = jnp.where(row <= col, 1.0, 0.0).astype(BF16)
    grad_a_ref[...] = dot(
        jnp.concatenate([upper] * 3, 1), jnp.concatenate(split3(grad_running), 0)
    )


def per_device(inputs, gate_input, log_decay, b_matrix, c_matrix, norm_gain, cotangent):
    tokens, width = inputs.shape
    heads = log_decay.shape[1]
    size = b_matrix.shape[2]
    blocks = tokens // SPAN
    full_width = width * lax.axis_size("head")
    b_half = b_matrix.reshape(tokens, size)
    c_half = c_matrix.reshape(tokens, size)
    gain = norm_gain.reshape(1, width)

    def rows(cols, height=SPAN):
        return pl.BlockSpec((height, cols), lambda k: (k, 0))

    def back(cols):
        return pl.BlockSpec((SPAN, cols), lambda k: (blocks - 1 - k, 0))

    def whole(*shape):
        return pl.BlockSpec(shape, lambda k: (0,) * len(shape))

    def shape(*dims, dtype=F32):
        return jax.ShapeDtypeStruct(dims, dtype)

    def call(kernel, in_specs, out_specs, out_shape, flops, moved, scratch=()):
        return pl.pallas_call(
            kernel,
            grid=(blocks,),
            in_specs=in_specs,
            out_specs=out_specs,
            out_shape=out_shape,
            scratch_shapes=list(scratch),
            compiler_params=pltpu.CompilerParams(
                dimension_semantics=("arbitrary",), vmem_limit_bytes=VMEM_BYTES
            ),
            cost_estimate=pl.CostEstimate(
                flops=flops, bytes_accessed=moved, transcendentals=0
            ),
        )

    mega = 1 << 20
    carry = pltpu.VMEM((size, width), F32)
    local, totals = call(
        local_state_kernel,
        [rows(width), rows(heads), rows(size)],
        [whole(size, width), whole(8, width)],
        [shape(size, width), shape(8, width)],
        600 * mega,
        3 * mega,
    )(inputs, log_decay, b_half)
    incoming = chain(local, totals, False)
    diagonal = call(
        diagonal_kernel,
        [rows(width), rows(heads), rows(size), rows(size)],
        rows(width),
        shape(tokens, width),
        5000 * mega,
        8 * mega,
    )(inputs, log_decay, b_half, c_half)
    ssd_out, states, sums = call(
        forward_kernel,
        [
            rows(width), rows(width), rows(heads), rows(size), rows(size), rows(width),
            rows(width), whole(1, width), whole(size, width),
        ],
        [rows(width), rows(width, size), rows(SPAN, 8)],
        [shape(tokens, width), shape(blocks * size, width), shape(blocks * 8, SPAN)],
        1500 * mega,
        20 * mega,
        [carry],
    )(diagonal, inputs, log_decay, b_half, c_half, gate_input, cotangent, gain, incoming)
    sums = lax.psum(sums, "head")
    normed, grad_gate, upstream, leaving = call(
        functools.partial(norm_kernel, full_width),
        [
            rows(width), rows(heads), rows(size), rows(width), rows(width),
            whole(1, width), rows(SPAN, 8),
        ],
        [rows(width), rows(width), rows(width), whole(size, width)],
        [
            shape(tokens, width, dtype=BF16), shape(tokens, width, dtype=BF16),
            shape(tokens, width), shape(size, width),
        ],
        1000 * mega,
        20 * mega,
        [pltpu.VMEM((8, width), F32)],
    )(ssd_out, log_decay, c_half, gate_input, cotangent, gain, sums)
    adjoint = chain(leaving, totals, True)
    diagonal_grad, part_b, part_c = call(
        diagonal_grad_kernel,
        [rows(width), rows(heads), rows(size), rows(size), rows(width)],
        [rows(width), rows(size), rows(size)],
        [shape(tokens, width), shape(tokens, size), shape(tokens, size)],
        8000 * mega,
        12 * mega,
    )(inputs, log_decay, b_half, c_half, upstream)
    grad_x, grad_a, grad_b, grad_c = call(
        backward_kernel,
        [
            back(width), back(heads), back(size), back(size), back(width), back(width),
            pl.BlockSpec((size, width), lambda k: (blocks - 1 - k, 0)), back(width),
            whole(size, width), back(size), back(size),
        ],
        [back(width), back(heads), back(size), back(size)],
        [
            shape(tokens, width, dtype=BF16), shape(tokens, heads),
            shape(tokens, size), shape(tokens, size),
        ],
        3000 * mega,
        30 * mega,
        [carry],
    )(
        inputs, log_decay, b_half, c_half, upstream, ssd_out, states, diagonal_grad,
        adjoint, part_b, part_c,
    )
    return (
        normed, grad_x, grad_gate, grad_a,
        grad_b.reshape(b_matrix.shape), grad_c.reshape(c_matrix.shape),
    )


def solution(mesh):
    wide = P("seq", "head")
    grouped = P("seq", "head", None)
    return jax.shard_map(
        per_device,
        mesh=mesh,
        in_specs=(wide, wide, wide, grouped, grouped, P("head"), wide),
        out_specs=(wide, wide, wide, wide, grouped, grouped),
        check_vma=False,
    )
```
